128 devices in a mesh: sec: 2 (over z_lo), grp: 4 (over z_hi, core), shard: 16 (over x, y).
Axes of the slice: x: 4, y: 4, z: 4 (z_hi: 2, z_lo: 2; z = z_hi * 2 + z_lo), core: 2. Of those that a mesh axis runs over, the one named last changes fastest.
Arguments:
- queries: bfloat16 [512, 8192], P(('sec', 'grp', 'shard')), may hold values from -10 to 10
- cache_keys: bfloat16 [512, 512, 512], P(('sec', 'grp', 'shard')), may hold values from -10 to 10
- cache_values: bfloat16 [512, 512, 512], P(('sec', 'grp', 'shard')), may hold values from -6 to 6
- new_keys: bfloat16 [512, 512], P(('sec', 'grp', 'shard')), may hold values from -6 to 6
- new_values: bfloat16 [512, 512], P(('sec', 'grp', 'shard')), may hold values from -6 to 6
- lengths: int32 [512], P(('sec', 'grp', 'shard')), may hold values from 1 to 512, 131072 in all
- out_weight: bfloat16 [8192, 16384], P('shard', ('sec', 'grp')), may hold values from -0.5 to 0.5
- residual: bfloat16 [512, 16384], P('shard', ('sec', 'grp')), may hold values from -30 to 30
- norm_gain: float32 [16384], P(('sec', 'grp')), may hold values from 0.5 to 2
- gate_up: bfloat16 [16384, 2, 26624], P(('sec', 'grp'), None, 'shard'), may hold values from -0.046875 to 0.046875
- down_weight: bfloat16 [26624, 16384], P('shard', ('sec', 'grp')), may hold values from -0.078125 to 0.078125
Outputs:
- mixed: bfloat16 [512, 16384], P('shard', ('sec', 'grp'))
The draws below stay inside these ranges and needn't reach their ends.
Inputs may be any that keep to these rules, and one draw needn't show every extreme that they name: Each row attends to its first lengths[r] cache slots and to its new token; some row has 512.
All inputs are finite; a program needn't handle non-finite values. No bound on the sum of `lengths` on one device may be relied on, other than what follows from the above.
Results may differ from the reference program's by a relative error of at most 0.011.
Values may be sent and summed in bfloat16 or wider, within the bound.
A program may use at most 128 MiB of HBM per device.

```python
import math
import jax
import jax.numpy as jnp
import numpy as np
from jax import lax

D = 16384
QH = 64
KVH = 4
HD = 128
FF = 26624
LEN = 512
ROWS = 512


def draw_queries(key, part):
    key = jax.random.fold_in(key, 11)
    values = jax.random.truncated_normal(key, -6.0, 6.0, (ROWS, QH * HD), jnp.float32)
    return values.astype(jnp.bfloat16)


def draw_cache_keys(key, part):
    key = jax.random.fold_in(key, 12)
    values = jax.random.truncated_normal(key, -6.0, 6.0, (ROWS, LEN, KVH * HD), jnp.float32)
    return values.astype(jnp.bfloat16)


def draw_residual(key, part):
    key = jax.random.fold_in(key, 7)
    first_key, second_key, third_key = jax.random.split(key, 3)
    row_scale = jnp.exp(jax.random.uniform(first_key, (ROWS, 1), jnp.float32, math.log(0.15), math.log(1.5)))
    column_scale = jnp.exp(jax.random.uniform(second_key, (1, D), jnp.float32, math.log(0.3), math.log(3.0)))
    values = jax.random.truncated_normal(third_key, -6.0, 6.0, (ROWS, D), jnp.float32)
    return (values * row_scale * column_scale).astype(jnp.bfloat16)


def shard_levels(rng, extent, shards, low, high):
    def one(dim, shards_of):
        draws = jax.random.uniform(jax.random.fold_in(jax.random.fold_in(rng, 6), dim), (shards_of,), jnp.float32, low / len(shards), high / len(shards))
        return jnp.repeat(jnp.exp(draws), extent[dim] // shards_of).reshape((-1,) + (1,) * (len(extent) - dim - 1))

    gain = one(*shards[0])
    for cut in shards[1:]:
        gain = gain * one(*cut)
    return gain


def split_up(count, total, limit, skew):
    loads = [(1 << 20) // math.isqrt(rank ** skew) + 1 for rank in range(2, count + 1)]
    spare, holding = total - limit - (count - 1), [1] * (count - 1)
    while spare > 0:
        free = [i for i in range(count - 1) if holding[i] < limit]
        mass, budget = sum([loads[i] for i in free]), spare
        for i in free:
            extra = min(limit - holding[i], max(1, budget * loads[i] // mass), spare)
            holding[i] = holding[i] + extra
            spare = spare - extra
    return np.array([limit] + holding)


def uneven(own_key, number_of, total, reach, lean):
    if number_of == 2:
        one = jax.random.randint(own_key, (), max(1, total - reach), min(reach, total - 1) + 1)
        return jnp.stack([one, total - one])
    sizes = jnp.asarray(split_up(number_of, total, reach, lean), jnp.int32)
    pairs = (number_of - 1) // 2
    donor, sink = sizes[1:1 + 2 * pairs:2], sizes[2:2 + 2 * pairs:2]
    room = jnp.minimum(donor - 1, reach - sink)
    moved = jax.random.randint(jax.random.fold_in(own_key, 1), (pairs,), 0, 1 << 20) % (room + 1)
    sizes = sizes.at[1:1 + 2 * pairs:2].set(donor - moved).at[2:2 + 2 * pairs:2].set(sink + moved)
    return sizes[jax.random.permutation(jax.random.fold_in(own_key, 2), number_of)]


def gaussian(stream_key, shape, scale, most, shards=(), kind=jnp.bfloat16):
    result = scale * jax.random.normal(stream_key, shape, jnp.float32)
    if shards:
        result = result * shard_levels(stream_key, shape, shards, -0.22, 0.18)
    return jnp.clip(result, -most, most).astype(kind)


def setup_inputs(seed: int = 0) -> dict:
    key_of = jax.random.split(jax.random.key(seed), 12)
    queries = draw_queries(jax.random.fold_in(key_of[11], 71), 0)
    cache_keys = draw_cache_keys(jax.random.fold_in(key_of[11], 71), 0)
    cache_values = gaussian(key_of[2], (ROWS, LEN, KVH * HD), 1.0, 6.0, ((0, 128),))
    new_keys = gaussian(key_of[3], (ROWS, KVH * HD), 1.0, 6.0, ((0, 128),))
    new_values = gaussian(key_of[4], (ROWS, KVH * HD), 1.0, 6.0, ((0, 128),))
    lengths = uneven(key_of[5], ROWS, ROWS * LEN // 2, LEN, 2).astype(jnp.int32)
    out_weight = gaussian(key_of[6], (QH * HD, D), HD ** -0.5, 0.5, ((0, 16), (1, 8)))
    residual = draw_residual(jax.random.fold_in(key_of[11], 71), 0)
    norm_gain = jnp.clip(jnp.exp(math.log(2.0) - 1.3862944 * jax.random.uniform(key_of[8], (D,), jnp.float32) ** shard_levels(key_of[8], (D,), ((0, 8),), -0.2, 0.2)), 0.5, 2.0)
    gate_up = gaussian(key_of[9], (D, 2, FF), D ** -0.5, 0.046875, ((0, 8), (2, 16)))
    down_weight = gaussian(key_of[10], (FF, D), (FF // 4) ** -0.5, 0.078125, ((0, 16), (1, 8)))
    return dict(queries=queries, cache_keys=cache_keys, cache_values=cache_values, new_keys=new_keys, new_values=new_values, lengths=lengths, out_weight=out_weight, residual=residual, norm_gain=norm_gain, gate_up=gate_up, down_weight=down_weight)


def attend_row(items):
    query, keys, values, key_new, value_new, count = items
    heads_per = QH // KVH
    scaling = HD ** (-0.5)
    query_heads = query.astype(jnp.float32).reshape(KVH, heads_per, HD)
    key_heads = keys.astype(jnp.float32).reshape(LEN, KVH, HD)
    value_heads = values.astype(jnp.float32).reshape(LEN, KVH, HD)
    scores = jnp.einsum('kgd,lkd->kgl', query_heads, key_heads) * scaling
    own_score = jnp.einsum('kgd,kd->kg', query_heads, key_new.astype(jnp.float32).reshape(KVH, HD)) * scaling
    usable = jnp.arange(LEN, dtype=jnp.int32) < count
    scores = jnp.where(usable[None, None, :], scores, -jnp.inf)
    highest = jnp.maximum(lax.optimization_barrier(jnp.max(scores, axis=-1)), own_score)
    weights = jnp.exp(scores - highest[..., None])
    own_weight = jnp.exp(own_score - highest)
    totals = lax.optimization_barrier(jnp.sum(weights, axis=-1)) + own_weight
    weights_low = lax.optimization_barrier(weights.astype(jnp.bfloat16)).astype(jnp.float32)
    own_low = lax.optimization_barrier(own_weight.astype(jnp.bfloat16)).astype(jnp.float32)
    numerator = jnp.einsum('kgl,lkd->kgd', weights_low, value_heads)
    numerator = numerator + own_low[..., None] * value_new.astype(jnp.float32).reshape(KVH, 1, HD)
    return (numerator / totals[..., None]).astype(jnp.bfloat16).reshape(QH * HD)

def reference(queries, cache_keys, cache_values, new_keys, new_values, lengths, out_weight, residual, norm_gain, gate_up, down_weight):
    attn = lax.map(attend_row, (queries, cache_keys, cache_values, new_keys, new_values, lengths))
    stream = residual.astype(jnp.float32) + jnp.dot(attn, out_weight, preferred_element_type=jnp.float32)
    mean_square = lax.optimization_barrier(jnp.mean(stream * stream, axis=1))
    normed = (stream * lax.rsqrt(mean_square + 1e-05)[:, None] * norm_gain[None, :]).astype(jnp.bfloat16)
    gate_and_up = jnp.dot(normed, gate_up.reshape(D, 2 * FF), preferred_element_type=jnp.float32)
    hidden = (jax.nn.silu(gate_and_up[:, :FF]) * gate_and_up[:, FF:]).astype(jnp.bfloat16)
    mixed = stream + jnp.dot(hidden, down_weight, preferred_element_type=jnp.float32)
    return mixed.astype(jnp.bfloat16)
```

```python
import jax
import jax.numpy as jnp
from jax import lax
from jax.experimental import pallas as pl
from jax.experimental.pallas import tpu as pltpu
from jax.sharding import PartitionSpec as P

MESH = pl.DeviceIdType.MESH
BF = jnp.bfloat16
F32 = jnp.float32

D = 16384
KVH = 4
HD = 128
LEN = 512
ROWS = 512
FEATURES = 2048
HIDDEN = 1664
EPSILON = 1e-05

CHUNKS = 2
R = 32 // CHUNKS
HALF = FEATURES // 2
TILE = 256
FIRST = 7 * TILE
PIECES = 4
LAG = 0

HALVES = (slice(0, HALF), slice(HALF, FEATURES))
GROUPS = (slice(0, FIRST), slice(FIRST, 2 * HIDDEN))


def kernel(
    lengths, queries, new_keys, new_values, residual, norm_gain,
    cache_keys, cache_values, out_weight, gate_up, down_weight,
    mixed,
    keys, values, wo, raw, gu, wd, q_rows, att, tiles, arrived, attn, unweave, regroup,
    part, part_in, slab, slab_in, rows, stream, squares, squares_in,
    gates, gates_core, gates_in, hidden,
    send_sem, recv_sem, local_sem,
):
    sec = lax.axis_index("sec")
    grp = lax.axis_index("grp")
    shard = lax.axis_index("shard")
    z = (grp // 2) * 2 + sec
    core = grp % 2
    x = shard // 4
    y = shard % 4
    block = sec * 4 + grp

    def plane(at):
        return {"shard": at}

    def along_x(d):
        return {"shard": ((x + d) % 4) * 4 + y}

    def along_y(d):
        return {"shard": x * 4 + (y + d) % 4}

    def along_z(d, other=False):
        to = (z + d) % 4
        c = 1 - core if other else core
        return {"sec": to % 2, "grp": (to // 2) * 2 + c}

    def across():
        return {"grp": (grp // 2) * 2 + (1 - core)}

    sent = []

    def send(src, dst, to):
        i = len(sent)
        copy = pltpu.make_async_remote_copy(
            src_ref=src, dst_ref=dst, send_sem=send_sem.at[i], recv_sem=recv_sem.at[i],
            device_id=to, device_id_type=MESH,
        )
        copy.start()
        sent.append(copy)
        return copy

    fetched = []

    def fetch(src, dst):
        copy = pltpu.make_async_copy(src, dst, local_sem.at[len(fetched)])
        copy.start()
        fetched.append(copy)
        return copy

    cache = [
        (fetch(cache_keys.at[r], keys.at[r]), fetch(cache_values.at[r], values.at[r]))
        for r in range(4)
    ]
    barrier = pltpu.get_barrier_semaphore()
    for d in range(1, 16):
        pl.semaphore_signal(barrier, inc=1, device_id=plane((shard + d) % 16), device_id_type=MESH)
    for d in range(1, 4):
        pl.semaphore_signal(barrier, inc=1, device_id=along_z(d), device_id_type=MESH)
        pl.semaphore_signal(barrier, inc=1, device_id=along_z(d, True), device_id_type=MESH)
    pl.semaphore_signal(barrier, inc=1, device_id=across(), device_id_type=MESH)

    wo_in = fetch(out_weight, wo)
    woven = gate_up.reshape(2 * FEATURES, HIDDEN)
    depth = 2 * FEATURES // PIECES

    def fetch_raw(p):
        return fetch(woven.at[pl.ds(p * depth, depth), :], raw.at[p % 2])

    raw_in = {0: fetch_raw(0), 1: fetch_raw(1)}
    wd_in = fetch(down_weight, wd)

    i = lax.broadcasted_iota(jnp.int32, (256, 256), 0)
    j = lax.broadcasted_iota(jnp.int32, (256, 256), 1)
    unweave[...] = jnp.where(j == (i % 128) * 2 + i // 128, 1.0, 0.0).astype(BF)
    regroup[...] = jnp.where(
        j == ((i % 64) // 4) * 16 + (i % 4) * 4 + i // 64, 1.0, 0.0
    ).astype(BF)

    def unweave_piece(p):
        raw_in[p].wait()

        def body(step, carry):
            at = pl.multiple_of(step * 256, 256)
            both = jnp.dot(
                unweave[...], raw[p % 2, pl.ds(at, 256), :], preferred_element_type=F32
            ).astype(BF)
            to = pl.ds(pl.multiple_of(p * (depth // 2) + step * 128, 128), 128)
            gu[to, 0:HIDDEN] = both[:128]
            gu[to, HIDDEN:] = both[128:]
            return carry

        lax.fori_loop(0, depth // 256, body, 0)
        if p + 2 < PIECES:
            raw_in[p + 2] = fetch_raw(p + 2)

    scaling = HD ** (-0.5)
    for h in range(KVH * 16):
        q_rows[:, h, :] = queries[:, h * HD:(h + 1) * HD].astype(F32)
    own_keys = new_keys[...].astype(F32)
    own_values = new_values[...].astype(F32)
    slots = lax.broadcasted_iota(jnp.int32, (1, LEN), 1)
    for r in range(4):
        cache[r][0].wait()
        cache[r][1].wait()
        usable = slots < lengths[r]
        for k in range(KVH):
            of_head = slice(k * HD, (k + 1) * HD)
            query = q_rows[r, k * 16:(k + 1) * 16, :]
            scores = lax.dot_general(
                query.astype(BF), keys[r, :, of_head], (((1,), (1,)), ((), ())),
                preferred_element_type=F32,
            ) * scaling
            own = jnp.sum(query * own_keys[r:r + 1, of_head], axis=1, keepdims=True) * scaling
            scores = jnp.where(usable, scores, -1e30)
            top = jnp.maximum(jnp.max(scores, axis=1, keepdims=True), own)
            weights = jnp.exp(scores - top)
            own_weight = jnp.exp(own - top)
            total = jnp.sum(weights, axis=1, keepdims=True) + own_weight
            summed = jnp.dot(
                weights.astype(BF), values[r, :, of_head], preferred_element_type=F32
            ) + own_weight.astype(BF).astype(F32) * own_values[r:r + 1, of_head]
            result = summed / total
            for g in range(4):
                att[4 * k + g, 4 * r:4 * r + 4, :] = result[4 * g:4 * g + 4, :]
    tiles[...] = att[...].astype(BF)

    pl.semaphore_wait(barrier, 22)

    exchange = []
    for d in range(1, 16):
        to = (shard + d) % 16
        exchange.append(send(tiles.at[to], arrived.at[shard], plane(to)))
    arrived[shard] = tiles[shard]
    unweave_piece(0)
    for copy in exchange:
        copy.wait_recv()
    grouped = jnp.dot(
        regroup[...], arrived[...].reshape(256, HD), preferred_element_type=F32
    ).astype(BF)
    for h in range(4):
        of_head = grouped[h * 64:(h + 1) * 64, :].reshape(2, CHUNKS, R, HD)
        for c in range(CHUNKS):
            attn[c, pl.ds(2 * block, 2), :, h * HD:(h + 1) * HD] = of_head[:, c]
    gather = []
    mine = attn.at[:, pl.ds(2 * block, 2)]
    for d in (2, 1, 3):
        gather.append(send(mine, mine, along_z(d)))
        gather.append(send(mine, mine, along_z(d, True)))
    gather.append(send(mine, mine, across()))
    unweave_piece(1)
    wo_in.wait()
    for copy in gather:
        copy.wait_recv()

    gain = norm_gain[...].reshape(1, FEATURES)
    unscale = 1.0 / (gain * gain)

    def product(c, lhs, weight, half, dst):
        start = half.start
        count = (half.stop - start) // TILE

        def body(step, carry):
            at = pl.ds(pl.multiple_of(start + step * TILE, TILE), TILE)
            tile = jnp.dot(
                lhs[...].reshape(16 * R, lhs.shape[-1]), weight[:, at],
                preferred_element_type=F32,
            ).astype(BF)
            dst[c, :, :, at] = tile.reshape(16, R, TILE)
            return carry

        lax.fori_loop(0, count, body, 0)

    def scatter_out(u, c, h):
        copies = []
        grid = part.at[u, c].reshape(4, 4, R, FEATURES)
        for n, d in enumerate((2, 1, 3)):
            if h == 0:
                src, to = grid.at[(x + d) % 4, :, :, HALVES[h]], along_x(d)
            else:
                src, to = grid.at[:, (y + d) % 4, :, HALVES[h]], along_y(d)
            copies.append(send(src, part_in.at[u, c, h, n], to))
        return copies

    def scatter_mid(u, c, h, copies):
        for copy in copies:
            copy.wait_recv()
        grid = part.at[u, c].reshape(4, 4, R, FEATURES)
        total = (grid[x, :, :, HALVES[h]] if h == 0 else grid[:, y, :, HALVES[h]]).astype(F32)
        for n in range(3):
            total = total + part_in[u, c, h, n].astype(F32)
        slab[u, c, h] = total.astype(BF)
        out = []
        for n, d in enumerate((2, 1, 3)):
            if h == 0:
                src, to = slab.at[u, c, h, (y + d) % 4], along_y(d)
            else:
                src, to = slab.at[u, c, h, (x + d) % 4], along_x(d)
            out.append(send(src, slab_in.at[u, c, h, n], to))
        return out

    def scatter_end(u, c, h, copies):
        for copy in copies:
            copy.wait_recv()
        total = slab[u, c, h, y if h == 0 else x].astype(F32)
        for n in range(3):
            total = total + slab_in[u, c, h, n].astype(F32)
        return total

    def chain(c):
        lhs = attn.at[c]
        first = []
        for h in (0, 1):
            product(c, lhs, wo, HALVES[h], part.at[0])
            first.append(scatter_out(0, c, h))
            yield
        second = []
        for h in (0, 1):
            second.append(scatter_mid(0, c, h, first[h]))
            yield
        gathers = []
        for h in (0, 1):
            cols = HALVES[h]
            value = residual[c * R:(c + 1) * R, cols].astype(F32) + scatter_end(0, c, h, second[h])
            stream[c, :, cols] = value
            rows[c, x, y, :, cols] = (value * gain[:, cols]).astype(BF)
            here = rows.at[c, x, y, :, cols]
            gathers.append([
                send(here, here, along_y(d) if h == 0 else along_x(d)) for d in (2, 1, 3)
            ])
        yield
        wider = []
        for h in (0, 1):
            for copy in gathers[h]:
                copy.wait_recv()
            here = rows.at[c, x, :, :, HALVES[h]] if h == 0 else rows.at[c, :, y, :, HALVES[h]]
            wider += [send(here, here, along_x(d) if h == 0 else along_y(d)) for d in (2, 1, 3)]
            yield
        for copy in wider:
            copy.wait_recv()

        def square(b, carry):
            v = rows[c, b // 4, b % 4].astype(F32)
            total = jnp.sum(v * v * unscale, axis=1, keepdims=True)
            squares[c, b] = jnp.broadcast_to(total, (R, 128))
            return carry

        lax.fori_loop(0, 16, square, 0)
        square_copies = []
        n = 0
        for other in (False, True):
            for d in (0, 1, 2, 3):
                if d == 0 and not other:
                    continue
                owner = (1 - core if other else core) * 4 + (z + d) % 4
                square_copies.append(send(
                    squares.at[c, pl.ds(2 * owner, 2)], squares_in.at[c, n],
                    across() if d == 0 else along_z(d, other),
                ))
                n += 1
        yield
        lhs = rows.at[c].reshape(16, R, FEATURES)
        crossing = []
        theirs = pl.ds(8 * (1 - core), 8)
        for g in (0, 1):
            product(c, lhs, gu, GROUPS[g], gates)
            crossing.append(send(
                gates.at[c, theirs, :, GROUPS[g]], gates_core.at[c, :, :, GROUPS[g]], across()
            ))
            yield
        reduced = []
        for g in (0, 1):
            crossing[g].wait_recv()
            for n, d in enumerate((2, 1, 3)):
                to = (z + d) % 4
                at = pl.ds(8 * core + 2 * to, 2)
                gates[c, at, :, GROUPS[g]] = (
                    gates[c, at, :, GROUPS[g]].astype(F32)
                    + gates_core[c, pl.ds(2 * to, 2), :, GROUPS[g]].astype(F32)
                ).astype(BF)
                reduced.append(send(
                    gates.at[c, at, :, GROUPS[g]], gates_in.at[c, n, :, :, GROUPS[g]], along_z(d)
                ))
            yield
        for copy in square_copies + reduced:
            copy.wait_recv()
        owner = 2 * (4 * core + z)
        total = squares[c, pl.ds(owner, 2)]
        for n in range(7):
            total = total + squares_in[c, n]
        scale = lax.rsqrt(total / D + EPSILON)[:, :, 0:1]

        def summed(cols):
            total = gates[c, pl.ds(owner, 2), :, cols].astype(F32)
            total = total + gates_core[c, pl.ds(2 * z, 2), :, cols].astype(F32)
            for n in range(3):
                total = total + gates_in[c, n, :, :, cols].astype(F32)
            return total * scale

        gate = summed(slice(0, HIDDEN))
        up = summed(slice(HIDDEN, 2 * HIDDEN))
        hidden[c, pl.ds(owner, 2)] = (gate / (1.0 + jnp.exp(-gate)) * up).astype(BF)
        here = hidden.at[c, pl.ds(owner, 2)]
        spread = [send(here, here, along_z(d)) for d in (2, 1, 3)]
        over = [send(here, here, across())]
        yield
        for d, copy in sorted(zip((2, 1, 3), spread), key=lambda e: e[0] == 2):
            copy.wait_recv()
            there = hidden.at[c, pl.ds(2 * (4 * core + (z - d + 4) % 4), 2)]
            over.append(send(there, there, across()))
        yield
        for copy in over:
            copy.wait_recv()
        lhs = hidden.at[c]
        first = []
        for h in (0, 1):
            product(c, lhs, wd, HALVES[h], part.at[1])
            first.append(scatter_out(1, c, h))
            yield
        second = []
        for h in (0, 1):
            second.append(scatter_mid(1, c, h, first[h]))
            yield
        for h in (0, 1):
            cols = HALVES[h]
            mixed[c * R:(c + 1) * R, cols] = (
                stream[c, :, cols] + scatter_end(1, c, h, second[h])
            ).astype(BF)

    chains = [chain(c) for c in range(CHUNKS)]
    done = [0] * CHUNKS
    live = [True] * CHUNKS
    rest = [lambda: unweave_piece(2), lambda: unweave_piece(3)]

    def advance(c):
        if live[c]:
            try:
                next(chains[c])
                done[c] += 1
            except StopIteration:
                live[c] = False

    turn = 0
    while any(live):
        for c in range(CHUNKS):
            if turn >= c * LAG:
                advance(c)
        turn += 1
        if turn == 2:
            for piece in rest:
                piece()
            wd_in.wait()
    for copy in sent:
        copy.wait_send()


SENDS = 15 + 7 + CHUNKS * (6 + 6 + 6 + 6 + 7 + 2 + 6 + 3 + 4 + 6 + 6)


def local(
    queries, cache_keys, cache_values, new_keys, new_values, lengths,
    out_weight, residual, norm_gain, gate_up, down_weight,
):
    vmem = pl.BlockSpec(memory_space=pltpu.VMEM)
    smem = pl.BlockSpec(memory_space=pltpu.SMEM)
    anywhere = pl.BlockSpec(memory_space=pl.ANY)
    return pl.pallas_call(
        kernel,
        out_shape=jax.ShapeDtypeStruct((32, FEATURES), BF),
        in_specs=[smem] + [vmem] * 5 + [anywhere] * 5,
        out_specs=vmem,
        scratch_shapes=[
            pltpu.VMEM((4, LEN, KVH * HD), BF),
            pltpu.VMEM((4, LEN, KVH * HD), BF),
            pltpu.VMEM((512, FEATURES), BF),
            pltpu.VMEM((2, 2 * FEATURES // PIECES, HIDDEN), BF),
            pltpu.VMEM((FEATURES, 2 * HIDDEN), BF),
            pltpu.VMEM((HIDDEN, FEATURES), BF),
            pltpu.VMEM((4, 64, HD), F32),
            pltpu.VMEM((16, 16, HD), F32),
            pltpu.VMEM((16, 16, HD), BF),
            pltpu.VMEM((16, 16, HD), BF),
            pltpu.VMEM((CHUNKS, 16, R, 512), BF),
            pltpu.VMEM((256, 256), BF),
            pltpu.VMEM((256, 256), BF),
            pltpu.VMEM((2, CHUNKS, 16, R, FEATURES), BF),
            pltpu.VMEM((2, CHUNKS, 2, 3, 4, R, HALF), BF),
            pltpu.VMEM((2, CHUNKS, 2, 4, R, HALF), BF),
            pltpu.VMEM((2, CHUNKS, 2, 3, R, HALF), BF),
            pltpu.VMEM((CHUNKS, 4, 4, R, FEATURES), BF),
            pltpu.VMEM((CHUNKS, R, FEATURES), F32),
            pltpu.VMEM((CHUNKS, 16, R, 128), F32),
            pltpu.VMEM((CHUNKS, 7, 2, R, 128), F32),
            pltpu.VMEM((CHUNKS, 16, R, 2 * HIDDEN), BF),
            pltpu.VMEM((CHUNKS, 8, R, 2 * HIDDEN), BF),
            pltpu.VMEM((CHUNKS, 3, 2, R, 2 * HIDDEN), BF),
            pltpu.VMEM((CHUNKS, 16, R, HIDDEN), BF),
            pltpu.SemaphoreType.DMA((SENDS,)),
            pltpu.SemaphoreType.DMA((SENDS,)),
            pltpu.SemaphoreType.DMA((8 + 2 + PIECES,)),
        ],
        compiler_params=pltpu.CompilerParams(
            collective_id=0, has_side_effects=True, vmem_limit_bytes=63 * 2**20,
        ),
        cost_estimate=pl.CostEstimate(
            flops=2 * 6 * 10**9, bytes_accessed=28 * 10**6, transcendentals=2 * 10**6
        ),
    )(
        lengths, queries, new_keys, new_values, residual, norm_gain,
        cache_keys, cache_values, out_weight, gate_up, down_weight,
    )


def solution(mesh):
    placed = (
        P(("sec", "grp", "shard"), None),
        P(("sec", "grp", "shard"), None, None),
        P(("sec", "grp", "shard"), None, None),
        P(("sec", "grp", "shard"), None),
        P(("sec", "grp", "shard"), None),
        P(("sec", "grp", "shard")),
        P("shard", ("sec", "grp")),
        P("shard", ("sec", "grp")),
        P(("sec", "grp")),
        P(("sec", "grp"), None, "shard"),
        P("shard", ("sec", "grp")),
    )
    return jax.shard_map(
        local, mesh=mesh, in_specs=placed, out_specs=P("shard", ("sec", "grp")), check_vma=False
    )
```

```python
import jax
import jax.numpy as jnp
from jax import lax
from jax.experimental import pallas as pl
from jax.experimental.pallas import tpu as pltpu
from jax.sharding import PartitionSpec as P

MESH = pl.DeviceIdType.MESH
BF = jnp.bfloat16
F32 = jnp.float32

D = 16384
KVH = 4
HD = 128
LEN = 512
ROWS = 512
FEATURES = 2048
HIDDEN = 1664
EPSILON = 1e-05

CHUNKS = 2
R = 32 // CHUNKS
HALF = FEATURES // 2
TILE = 256
PIECES = 4
ORDER = (
    (0, "out3"), (1, "attn"), (0, "mid1"), (1, "out1"), (0, "stream1"), (1, "mid1"), (0, "wide1"),
    (1, "stream1"), (0, "wide3"), (0, "unweave"), (1, "wide1"), (0, "gate0"), (1, "wide3"),
    (0, "gate3"), (1, "rows"), (0, "reduce2"), (1, "gate0"), (0, "squares"), (1, "squares"),
    (0, "hidden"), (1, "hidden"), (0, "down2"), (1, "onward"), (0, "down3"), (1, "down3"),
    (0, "downmid0"), (1, "downmid0"), (0, "downmid1"), (1, "downmid1"), (0, "downmid3"),
    (1, "end0"), (0, "end1"), (1, "end2"), (0, "end3"), (1, "end3"),
)

WIDE = HALF // 2
SPLIT = tuple((h, slice(h * HALF + q * WIDE, h * HALF + (q + 1) * WIDE)) for q in (0, 1) for h in (0, 1))
GROUPS = (slice(0, 1024), slice(1024, 1792), slice(1792, 2560), slice(2560, 2 * HIDDEN))


def kernel(
    lengths, queries, new_keys, new_values, norm_gain, residual,
    cache_keys, cache_values, out_weight, gate_up, down_weight,
    mixed,
    keys, values, residual_rows, wo, raw, gu, wd, q_rows, att, tiles, arrived, attn, unweave, regroup,
    part, part_in, slab, slab_in, rows, stream, squares, squares_in,
    gates, gates_core, gates_in, hidden,
    send_sem, recv_sem, local_sem,
):
    sec = lax.axis_index("sec")
    grp = lax.axis_index("grp")
    shard = lax.axis_index("shard")
    z = (grp // 2) * 2 + sec
    core = grp % 2
    x = shard // 4
    y = shard % 4
    block = sec * 4 + grp

    def plane(at):
        return {"shard": at}

    def along_x(d):
        return {"shard": ((x + d) % 4) * 4 + y}

    def along_y(d):
        return {"shard": x * 4 + (y + d) % 4}

    def along_z(d, other=False):
        to = (z + d) % 4
        c = 1 - core if other else core
        return {"sec": to % 2, "grp": (to // 2) * 2 + c}

    def across():
        return {"grp": (grp // 2) * 2 + (1 - core)}

    sent = []

    def send(src, dst, to):
        i = len(sent)
        copy = pltpu.make_async_remote_copy(
            src_ref=src, dst_ref=dst, send_sem=send_sem.at[i], recv_sem=recv_sem.at[i],
            device_id=to, device_id_type=MESH,
        )
        copy.start()
        sent.append(copy)
        return copy

    fetched = []

    def fetch(src, dst):
        copy = pltpu.make_async_copy(src, dst, local_sem.at[len(fetched)])
        copy.start()
        fetched.append(copy)
        return copy

    cache = [
        (fetch(cache_keys.at[r], keys.at[r]), fetch(cache_values.at[r], values.at[r]))
        for r in range(4)
    ]
    barrier = pltpu.get_barrier_semaphore()
    for d in range(1, 16):
        pl.semaphore_signal(barrier, inc=1, device_id=plane((shard + d) % 16), device_id_type=MESH)
    for d in range(1, 4):
        pl.semaphore_signal(barrier, inc=1, device_id=along_z(d), device_id_type=MESH)
        pl.semaphore_signal(barrier, inc=1, device_id=along_z(d, True), device_id_type=MESH)
    pl.semaphore_signal(barrier, inc=1, device_id=across(), device_id_type=MESH)

    woven = gate_up.reshape(2 * FEATURES, HIDDEN)
    depth = 2 * FEATURES // PIECES

    def fetch_raw(p):
        return fetch(woven.at[pl.ds(p * depth, depth), :], raw.at[p % 2])

    i = lax.broadcasted_iota(jnp.int32, (256, 256), 0)
    j = lax.broadcasted_iota(jnp.int32, (256, 256), 1)
    unweave[...] = jnp.where(j == (i % 128) * 2 + i // 128, 1.0, 0.0).astype(BF)
    regroup[...] = jnp.where(
        j == ((i % 64) // 4) * 16 + (i % 4) * 4 + i // 64, 1.0, 0.0
    ).astype(BF)

    def unweave_piece(p):
        raw_in[p].wait()

        def body(step, carry):
            at = pl.multiple_of(step * 256, 256)
            both = jnp.dot(
                unweave[...], raw[p % 2, pl.ds(at, 256), :], preferred_element_type=F32
            ).astype(BF)
            to = pl.ds(pl.multiple_of(p * (depth // 2) + step * 128, 128), 128)
            gu[to, 0:HIDDEN] = both[:128]
            gu[to, HIDDEN:] = both[128:]
            return carry

        lax.fori_loop(0, depth // 256, body, 0)
        if p + 2 < PIECES:
            raw_in[p + 2] = fetch_raw(p + 2)
        if p + 3 == PIECES:
            raw_in[PIECES] = fetch(down_weight, wd)

    scaling = HD ** (-0.5)
    for h in range(KVH * 16):
        q_rows[:, h, :] = queries[:, h * HD:(h + 1) * HD].astype(F32)
    own_keys = new_keys[...].astype(F32)
    own_values = new_values[...].astype(F32)
    slots = lax.broadcasted_iota(jnp.int32, (1, LEN), 1)
    for r in range(4):
        usable = slots < lengths[r]
        cache[r][0].wait()
        scores, own, own_value = [], [], []
        for k in range(KVH):
            of_head = slice(k * HD, (k + 1) * HD)
            query = q_rows[r, k * 16:(k + 1) * 16, :]
            scores.append(lax.dot_general(
                query.astype(BF), keys[r, :, of_head], (((1,), (1,)), ((), ())),
                preferred_element_type=F32,
            ))
            own.append(query * own_keys[r:r + 1, of_head])
            own_value.append(jnp.broadcast_to(own_values[r:r + 1, of_head], (16, HD)))
        scores = jnp.where(usable, jnp.concatenate(scores, axis=0) * scaling, -1e30)
        own = jnp.sum(jnp.concatenate(own, axis=0), axis=1, keepdims=True) * scaling
        top = jnp.maximum(jnp.max(scores, axis=1, keepdims=True), own)
        weights = jnp.exp(scores - top)
        own_weight = jnp.exp(own - top)
        total = jnp.sum(weights, axis=1, keepdims=True) + own_weight
        weights = weights.astype(BF)
        cache[r][1].wait()
        summed = jnp.concatenate([
            jnp.dot(
                weights[k * 16:(k + 1) * 16], values[r, :, k * HD:(k + 1) * HD],
                preferred_element_type=F32,
            ) for k in range(KVH)
        ], axis=0)
        own_low = own_weight.astype(BF).astype(F32)
        result = (summed + own_low * jnp.concatenate(own_value, axis=0)) / total
        for g in range(16):
            att[g, 4 * r:4 * r + 4, :] = result[4 * g:4 * g + 4, :]
    tiles[...] = att[...].astype(BF)

    wo_in = fetch(out_weight, wo)
    residual_in = fetch(residual, residual_rows)
    raw_in = {0: fetch_raw(0), 1: fetch_raw(1)}
    pl.semaphore_wait(barrier, 22)

    exchange = []
    for d in range(1, 16):
        to = (shard + d) % 16
        exchange.append(send(tiles.at[to], arrived.at[shard], plane(to)))
    arrived[shard] = tiles[shard]
    unweave_piece(0)
    for copy in exchange:
        copy.wait_recv()
    grouped = jnp.dot(
        regroup[...], arrived[...].reshape(256, HD), preferred_element_type=F32
    ).astype(BF)
    for h in range(4):
        of_head = grouped[h * 64:(h + 1) * 64, :].reshape(2, CHUNKS, R, HD)
        for c in range(CHUNKS):
            attn[c, pl.ds(2 * block, 2), :, h * HD:(h + 1) * HD] = of_head[:, c]
    spreads = []
    for c in range(CHUNKS):
        mine = attn.at[c, pl.ds(2 * block, 2)]
        spreads.append([send(mine, mine, along_z(d)) for d in (1, 3, 2)])
        spreads[c].append(send(mine, mine, across()))
    unweave_piece(1)
    wo_in.wait()
    residual_in.wait()

    gain = norm_gain[...].reshape(1, FEATURES)
    unscale = 1.0 / (gain * gain)

    def product(c, lhs, weight, half, dst):
        start = half.start
        count = (half.stop - start) // TILE

        def body(step, carry):
            at = pl.ds(pl.multiple_of(start + step * TILE, TILE), TILE)
            tile = jnp.dot(
                lhs[...].reshape(16 * R, lhs.shape[-1]), weight[:, at],
                preferred_element_type=F32,
            ).astype(BF)
            dst[c, :, :, at] = tile.reshape(16, R, TILE)
            return carry

        lax.fori_loop(0, count, body, 0)

    def scatter_out(u, c, p):
        h, cols = SPLIT[p]
        copies = []
        grid = part.at[u, c].reshape(4, 4, R, FEATURES)
        for n, d in enumerate((2, 1, 3)):
            if h == 0:
                src, to = grid.at[(x + d) % 4, :, :, cols], along_x(d)
            else:
                src, to = grid.at[:, (y + d) % 4, :, cols], along_y(d)
            copies.append(send(src, part_in.at[u, c, p, n], to))
        return copies

    def scatter_mid(u, c, p, copies):
        h, cols = SPLIT[p]
        for copy in copies:
            copy.wait_recv()
        grid = part.at[u, c].reshape(4, 4, R, FEATURES)
        total = (grid[x, :, :, cols] if h == 0 else grid[:, y, :, cols]).astype(F32)
        for n in range(3):
            total = total + part_in[u, c, p, n].astype(F32)
        slab[u, c, p] = total.astype(BF)
        out = []
        for n, d in enumerate((2, 1, 3)):
            if h == 0:
                src, to = slab.at[u, c, p, (y + d) % 4], along_y(d)
            else:
                src, to = slab.at[u, c, p, (x + d) % 4], along_x(d)
            out.append(send(src, slab_in.at[u, c, p, n], to))
        return out

    def scatter_end(u, c, p, copies):
        for copy in copies:
            copy.wait_recv()
        total = slab[u, c, p, y if SPLIT[p][0] == 0 else x].astype(F32)
        for n in range(3):
            total = total + slab_in[u, c, p, n].astype(F32)
        return total

    def chain(c):
        over = [spreads[c].pop()]
        for d, copy in zip((1, 3, 2), spreads[c]):
            copy.wait_recv()
            from_z = (z - d + 4) % 4
            there = attn.at[c, pl.ds(2 * ((from_z % 2) * 4 + (from_z // 2) * 2 + core), 2)]
            over.append(send(there, there, across()))
        yield "attn"
        for copy in over:
            copy.wait_recv()
        lhs = attn.at[c]
        first = []
        for p, (h, cols) in enumerate(SPLIT):
            product(c, lhs, wo, cols, part.at[0])
            first.append(scatter_out(0, c, p))
            yield f"out{p}"
        second = []
        for p in range(4):
            second.append(scatter_mid(0, c, p, first[p]))
            yield f"mid{p}"
        gathers = []
        for p, (h, cols) in enumerate(SPLIT):
            value = residual_rows[c * R:(c + 1) * R, cols].astype(F32) + scatter_end(0, c, p, second[p])
            stream[c, :, cols] = value
            rows[c, x, y, :, cols] = (value * gain[:, cols]).astype(BF)
            here = rows.at[c, x, y, :, cols]
            gathers.append([
                send(here, here, along_y(d) if h == 0 else along_x(d)) for d in (2, 1, 3)
            ])
            yield f"stream{p}"
        wider = []
        for p, (h, cols) in enumerate(SPLIT):
            for copy in gathers[p]:
                copy.wait_recv()
            here = rows.at[c, x, :, :, cols] if h == 0 else rows.at[c, :, y, :, cols]
            wider += [send(here, here, along_x(d) if h == 0 else along_y(d)) for d in (2, 1, 3)]
            yield f"wide{p}"
        for copy in wider:
            copy.wait_recv()
        yield "rows"

        lhs = rows.at[c].reshape(16, R, FEATURES)
        crossing = []
        reduced = []
        theirs = pl.ds(8 * (1 - core), 8)

        def cross(g):
            product(c, lhs, gu, GROUPS[g], gates)
            crossing.append(send(
                gates.at[c, theirs, :, GROUPS[g]], gates_core.at[c, :, :, GROUPS[g]], across()
            ))

        def reduce(g):
            crossing[g].wait_recv()
            for n, d in enumerate((2, 1, 3)):
                to = (z + d) % 4
                at = pl.ds(8 * core + 2 * to, 2)
                gates[c, at, :, GROUPS[g]] = (
                    gates[c, at, :, GROUPS[g]].astype(F32)
                    + gates_core[c, pl.ds(2 * to, 2), :, GROUPS[g]].astype(F32)
                ).astype(BF)
                reduced.append(send(
                    gates.at[c, at, :, GROUPS[g]], gates_in.at[c, n, :, :, GROUPS[g]], along_z(d)
                ))

        cross(0)
        yield "gate0"
        for g in range(1, len(GROUPS)):
            cross(g)
            yield f"gate{g}"
            reduce(g - 1)
            yield f"reduce{g - 1}"
        reduce(len(GROUPS) - 1)

        def square(b, carry):
            v = rows[c, b // 4, b % 4].astype(F32)
            total = jnp.sum(v * v * unscale, axis=1, keepdims=True)
            squares[c, b] = jnp.broadcast_to(total, (R, 128))
            return carry

        lax.fori_loop(0, 16, square, 0)
        square_copies = []
        n = 0
        for other in (False, True):
            for d in (0, 1, 2, 3):
                if d == 0 and not other:
                    continue
                owner = (1 - core if other else core) * 4 + (z + d) % 4
                square_copies.append(send(
                    squares.at[c, pl.ds(2 * owner, 2)], squares_in.at[c, n],
                    across() if d == 0 else along_z(d, other),
                ))
                n += 1
        yield "squares"
        for copy in square_copies + reduced:
            copy.wait_recv()
        owner = 2 * (4 * core + z)
        total = squares[c, pl.ds(owner, 2)]
        for n in range(7):
            total = total + squares_in[c, n]
        scale = lax.rsqrt(total / D + EPSILON)[:, :, 0:1]

        def summed(cols):
            total = gates[c, pl.ds(owner, 2), :, cols].astype(F32)
            total = total + gates_core[c, pl.ds(2 * z, 2), :, cols].astype(F32)
            for n in range(3):
                total = total + gates_in[c, n, :, :, cols].astype(F32)
            return total * scale

        gate = summed(slice(0, HIDDEN))
        up = summed(slice(HIDDEN, 2 * HIDDEN))
        hidden[c, pl.ds(owner, 2)] = (gate / (1.0 + jnp.exp(-gate)) * up).astype(BF)
        here = hidden.at[c, pl.ds(owner, 2)]
        spread = [send(here, here, along_z(d)) for d in (2, 1, 3)]
        over = [send(here, here, across())]
        yield "hidden"
        for d, copy in ((1, spread[1]), (3, spread[2]), (2, spread[0])):
            copy.wait_recv()
            there = hidden.at[c, pl.ds(2 * (4 * core + (z - d + 4) % 4), 2)]
            over.append(send(there, there, across()))
            if d != 1:
                yield "onward" if d == 3 else "over"
        for copy in over:
            copy.wait_recv()
        lhs = hidden.at[c]
        first = []
        for p, (h, cols) in enumerate(SPLIT):
            product(c, lhs, wd, cols, part.at[1])
            first.append(scatter_out(1, c, p))
            yield f"down{p}"
        second = []
        for p in range(4):
            second.append(scatter_mid(1, c, p, first[p]))
            yield f"downmid{p}"
        for p, (h, cols) in enumerate(SPLIT):
            mixed[c * R:(c + 1) * R, cols] = (
                stream[c, :, cols] + scatter_end(1, c, p, second[p])
            ).astype(BF)
            yield f"end{p}"

    chains = [chain(c) for c in range(CHUNKS)]
    for c, last in ORDER:
        if last == "unweave":
            unweave_piece(2)
            unweave_piece(3)
            raw_in[PIECES].wait()
            continue
        while next(chains[c]) != last:
            pass
    for copy in sent:
        copy.wait_send()


SENDS = 15 + CHUNKS * (7 + 6 * 12 + 7 + 16 + 7)


def local(
    queries, cache_keys, cache_values, new_keys, new_values, lengths,
    out_weight, residual, norm_gain, gate_up, down_weight,
):
    vmem = pl.BlockSpec(memory_space=pltpu.VMEM)
    smem = pl.BlockSpec(memory_space=pltpu.SMEM)
    anywhere = pl.BlockSpec(memory_space=pl.ANY)
    return pl.pallas_call(
        kernel,
        out_shape=jax.ShapeDtypeStruct((32, FEATURES), BF),
        in_specs=[smem] + [vmem] * 4 + [anywhere] * 6,
        out_specs=vmem,
        scratch_shapes=[
            pltpu.VMEM((4, LEN, KVH * HD), BF),
            pltpu.VMEM((4, LEN, KVH * HD), BF),
            pltpu.VMEM((32, FEATURES), BF),
            pltpu.VMEM((512, FEATURES), BF),
            pltpu.VMEM((2, 2 * FEATURES // PIECES, HIDDEN), BF),
            pltpu.VMEM((FEATURES, 2 * HIDDEN), BF),
            pltpu.VMEM((HIDDEN, FEATURES), BF),
            pltpu.VMEM((4, 64, HD), F32),
            pltpu.VMEM((16, 16, HD), F32),
            pltpu.VMEM((16, 16, HD), BF),
            pltpu.VMEM((16, 16, HD), BF),
            pltpu.VMEM((CHUNKS, 16, R, 512), BF),
            pltpu.VMEM((256, 256), BF),
            pltpu.VMEM((256, 256), BF),
            pltpu.VMEM((2, CHUNKS, 16, R, FEATURES), BF),
            pltpu.VMEM((2, CHUNKS, 4, 3, 4, R, WIDE), BF),
            pltpu.VMEM((2, CHUNKS, 4, 4, R, WIDE), BF),
            pltpu.VMEM((2, CHUNKS, 4, 3, R, WIDE), BF),
            pltpu.VMEM((CHUNKS, 4, 4, R, FEATURES), BF),
            pltpu.VMEM((CHUNKS, R, FEATURES), F32),
            pltpu.VMEM((CHUNKS, 16, R, 128), F32),
            pltpu.VMEM((CHUNKS, 7, 2, R, 128), F32),
            pltpu.VMEM((CHUNKS, 16, R, 2 * HIDDEN), BF),
            pltpu.VMEM((CHUNKS, 8, R, 2 * HIDDEN), BF),
            pltpu.VMEM((CHUNKS, 3, 2, R, 2 * HIDDEN), BF),
            pltpu.VMEM((CHUNKS, 16, R, HIDDEN), BF),
            pltpu.SemaphoreType.DMA((SENDS,)),
            pltpu.SemaphoreType.DMA((SENDS,)),
            pltpu.SemaphoreType.DMA((8 + 3 + PIECES,)),
        ],
        compiler_params=pltpu.CompilerParams(
            collective_id=0, has_side_effects=True, vmem_limit_bytes=63 * 2**20,
        ),
        cost_estimate=pl.CostEstimate(
            flops=2 * 6 * 10**9, bytes_accessed=28 * 10**6, transcendentals=2 * 10**6
        ),
    )(
        lengths, queries, new_keys, new_values, norm_gain, residual,
        cache_keys, cache_values, out_weight, gate_up, down_weight,
    )


def solution(mesh):
    placed = (
        P(("sec", "grp", "shard"), None),
        P(("sec", "grp", "shard"), None, None),
        P(("sec", "grp", "shard"), None, None),
        P(("sec", "grp", "shard"), None),
        P(("sec", "grp", "shard"), None),
        P(("sec", "grp", "shard")),
        P("shard", ("sec", "grp")),
        P("shard", ("sec", "grp")),
        P(("sec", "grp")),
        P(("sec", "grp"), None, "shard"),
        P("shard", ("sec", "grp")),
    )
    return jax.shard_map(
        local, mesh=mesh, in_specs=placed, out_specs=P("shard", ("sec", "grp")), check_vma=False
    )
```

```python
import jax
import jax.numpy as jnp
from jax import lax
from jax.experimental import pallas as pl
from jax.experimental.pallas import tpu as pltpu
from jax.sharding import PartitionSpec as P

MESH = pl.DeviceIdType.MESH
BF = jnp.bfloat16
F32 = jnp.float32

D = 16384
KVH = 4
HD = 128
LEN = 512
ROWS = 512
FEATURES = 2048
HIDDEN = 1664
EPSILON = 1e-05

CHUNKS = 2
R = 32 // CHUNKS
HALF = FEATURES // 2
TILE = 256
PIECES = 4
ORDER = (
    (0, "out3"), (1, "attn"), (0, "mid1"), (1, "out1"), (0, "stream1"), (1, "mid1"), (0, "wide1"),
    (1, "stream1"), (0, "wide3"), (0, "unweave"), (1, "wide1"), (0, "gate0"), (1, "wide3"),
    (0, "gate3"), (1, "rows"), (0, "reduce2"), (1, "gate0"), (0, "squares"), (1, "squares"),
    (0, "hidden"), (1, "hidden"), (0, "down2"), (1, "onward"), (0, "down3"), (1, "down3"),
    (0, "downmid0"), (1, "downmid0"), (0, "downmid1"), (1, "downmid1"), (0, "downmid3"),
    (1, "end0"), (0, "end1"), (1, "end2"), (0, "end3"), (1, "end3"),
)

WIDE = HALF // 2
SPLIT = tuple((h, slice(h * HALF + q * WIDE, h * HALF + (q + 1) * WIDE)) for q in (0, 1) for h in (0, 1))
GROUPS = (slice(0, 1024), slice(1024, 1792), slice(1792, 2560), slice(2560, 2 * HIDDEN))


def kernel(
    lengths, queries, new_keys, new_values, norm_gain, residual,
    cache_keys, cache_values, out_weight, gate_up, down_weight,
    mixed,
    keys, values, residual_rows, wo, raw, gu, wd, q_rows, att, tiles, arrived, attn, unweave, regroup,
    part, part_in, slab, slab_in, rows, stream, squares, squares_in,
    gates, gates_core, gates_in, hidden,
    send_sem, recv_sem, local_sem,
):
    sec = lax.axis_index("sec")
    grp = lax.axis_index("grp")
    shard = lax.axis_index("shard")
    z = (grp // 2) * 2 + sec
    core = grp % 2
    x = shard // 4
    y = shard % 4
    block = sec * 4 + grp

    def plane(at):
        return {"shard": at}

    def along_x(d):
        return {"shard": ((x + d) % 4) * 4 + y}

    def along_y(d):
        return {"shard": x * 4 + (y + d) % 4}

    def along_z(d, other=False):
        to = (z + d) % 4
        c = 1 - core if other else core
        return {"sec": to % 2, "grp": (to // 2) * 2 + c}

    def across():
        return {"grp": (grp // 2) * 2 + (1 - core)}

    sent = []
    groups = []

    def group():
        groups.append(len(groups))
        return groups[-1]

    def send(src, dst, to, i=None):
        i = group() if i is None else i
        copy = pltpu.make_async_remote_copy(
            src_ref=src, dst_ref=dst, send_sem=send_sem.at[len(sent) % SEND_SEMS],
            recv_sem=recv_sem.at[i], device_id=to, device_id_type=MESH,
        )
        copy.start()
        sent.append(copy)
        return copy

    def settle(ref, i):
        pltpu.make_async_copy(ref, ref, recv_sem.at[i]).wait()

    fetched = []

    def fetch(src, dst):
        copy = pltpu.make_async_copy(src, dst, local_sem.at[len(fetched)])
        copy.start()
        fetched.append(copy)
        return copy

    cache = [
        (fetch(cache_keys.at[r], keys.at[r]), fetch(cache_values.at[r], values.at[r]))
        for r in range(4)
    ]
    barrier = pltpu.get_barrier_semaphore()
    for d in range(1, 16):
        pl.semaphore_signal(barrier, inc=1, device_id=plane((shard + d) % 16), device_id_type=MESH)
    for d in range(1, 4):
        pl.semaphore_signal(barrier, inc=1, device_id=along_z(d), device_id_type=MESH)
        pl.semaphore_signal(barrier, inc=1, device_id=along_z(d, True), device_id_type=MESH)
    pl.semaphore_signal(barrier, inc=1, device_id=across(), device_id_type=MESH)

    woven = gate_up.reshape(2 * FEATURES, HIDDEN)
    depth = 2 * FEATURES // PIECES

    def fetch_raw(p):
        return fetch(woven.at[pl.ds(p * depth, depth), :], raw.at[p % 2])

    def unweave_piece(p):
        raw_in[p].wait()

        def body(step, carry):
            at = pl.multiple_of(step * 256, 256)
            both = jnp.dot(
                unweave[...], raw[p % 2, pl.ds(at, 256), :], preferred_element_type=F32
            ).astype(BF)
            to = pl.ds(pl.multiple_of(p * (depth // 2) + step * 128, 128), 128)
            gu[to, 0:HIDDEN] = both[:128]
            gu[to, HIDDEN:] = both[128:]
            return carry

        lax.fori_loop(0, depth // 256, body, 0)
        if p + 2 < PIECES:
            raw_in[p + 2] = fetch_raw(p + 2)
        if p + 3 == PIECES:
            raw_in[PIECES] = fetch(down_weight, wd)

    scaling = HD ** (-0.5)
    for h in range(KVH * 16):
        q_rows[:, h, :] = queries[:, h * HD:(h + 1) * HD].astype(F32)
    own_keys = new_keys[...].astype(F32)
    own_values = new_values[...].astype(F32)
    slots = lax.broadcasted_iota(jnp.int32, (1, LEN), 1)
    for r in range(4):
        usable = slots < lengths[r]
        cache[r][0].wait()
        scores, own, own_value = [], [], []
        for k in range(KVH):
            of_head = slice(k * HD, (k + 1) * HD)
            query = q_rows[r, k * 16:(k + 1) * 16, :]
            scores.append(lax.dot_general(
                query.astype(BF), keys[r, :, of_head], (((1,), (1,)), ((), ())),
                preferred_element_type=F32,
            ))
            own.append(query * own_keys[r:r + 1, of_head])
            own_value.append(jnp.broadcast_to(own_values[r:r + 1, of_head], (16, HD)))
        scores = jnp.where(usable, jnp.concatenate(scores, axis=0) * scaling, -1e30)
        own = jnp.sum(jnp.concatenate(own, axis=0), axis=1, keepdims=True) * scaling
        top = jnp.maximum(jnp.max(scores, axis=1, keepdims=True), own)
        weights = jnp.exp(scores - top)
        own_weight = jnp.exp(own - top)
        total = jnp.sum(weights, axis=1, keepdims=True) + own_weight
        weights = weights.astype(BF)
        cache[r][1].wait()
        summed = jnp.concatenate([
            jnp.dot(
                weights[k * 16:(k + 1) * 16], values[r, :, k * HD:(k + 1) * HD],
                preferred_element_type=F32,
            ) for k in range(KVH)
        ], axis=0)
        own_low = own_weight.astype(BF).astype(F32)
        result = (summed + own_low * jnp.concatenate(own_value, axis=0)) / total
        for g in range(16):
            att[g, 4 * r:4 * r + 4, :] = result[4 * g:4 * g + 4, :]
    tiles[...] = att[...].astype(BF)

    wo_in = fetch(out_weight, wo)
    residual_in = fetch(residual, residual_rows)
    raw_in = {0: fetch_raw(0), 1: fetch_raw(1)}
    pl.semaphore_wait(barrier, 22)

    exchange = group()
    for d in range(1, 16):
        to = (shard + d) % 16
        send(tiles.at[to], arrived.at[shard], plane(to), exchange)
    arrived[shard] = tiles[shard]
    i = lax.broadcasted_iota(jnp.int32, (256, 256), 0)
    j = lax.broadcasted_iota(jnp.int32, (256, 256), 1)
    regroup[...] = jnp.where(
        j == ((i & 60) << 2) + ((i & 3) << 2) + (i >> 6), 1.0, 0.0
    ).astype(BF)
    unweave[...] = jnp.where(j == ((i & 127) << 1) + (i >> 7), 1.0, 0.0).astype(BF)
    unweave_piece(0)
    settle(arrived.at[pl.ds(0, 15)], exchange)
    grouped = jnp.dot(
        regroup[...], arrived[...].reshape(256, HD), preferred_element_type=F32
    ).astype(BF)
    for h in range(4):
        of_head = grouped[h * 64:(h + 1) * 64, :].reshape(2, CHUNKS, R, HD)
        for c in range(CHUNKS):
            attn[c, pl.ds(2 * block, 2), :, h * HD:(h + 1) * HD] = of_head[:, c]
    spreads = []
    for c in range(CHUNKS):
        mine = attn.at[c, pl.ds(2 * block, 2)]
        spreads.append([send(mine, mine, along_z(d)) for d in (1, 3, 2)])
        spreads[c].append(group())
        send(mine, mine, across(), spreads[c][-1])
    unweave_piece(1)
    wo_in.wait()
    residual_in.wait()

    gain = norm_gain[...].reshape(1, FEATURES)
    unscale = 1.0 / (gain * gain)

    def product(c, lhs, weight, half, dst):
        start = half.start
        count = (half.stop - start) // TILE

        def body(step, carry):
            at = pl.ds(pl.multiple_of(start + step * TILE, TILE), TILE)
            tile = jnp.dot(
                lhs[...].reshape(16 * R, lhs.shape[-1]), weight[:, at],
                preferred_element_type=F32,
            ).astype(BF)
            dst[c, :, :, at] = tile.reshape(16, R, TILE)
            return carry

        lax.fori_loop(0, count, body, 0)

    def scatter_out(u, c, p):
        h, cols = SPLIT[p]
        i = group()
        grid = part.at[u, c].reshape(4, 4, R, FEATURES)
        for n, d in enumerate((2, 1, 3)):
            if h == 0:
                src, to = grid.at[(x + d) % 4, :, :, cols], along_x(d)
            else:
                src, to = grid.at[:, (y + d) % 4, :, cols], along_y(d)
            send(src, part_in.at[u, c, p, n], to, i)
        return i

    def scatter_mid(u, c, p, i):
        h, cols = SPLIT[p]
        settle(part_in.at[u, c, p], i)
        grid = part.at[u, c].reshape(4, 4, R, FEATURES)
        total = (grid[x, :, :, cols] if h == 0 else grid[:, y, :, cols]).astype(F32)
        for n in range(3):
            total = total + part_in[u, c, p, n].astype(F32)
        slab[u, c, p] = total.astype(BF)
        i = group()
        for n, d in enumerate((2, 1, 3)):
            if h == 0:
                src, to = slab.at[u, c, p, (y + d) % 4], along_y(d)
            else:
                src, to = slab.at[u, c, p, (x + d) % 4], along_x(d)
            send(src, slab_in.at[u, c, p, n], to, i)
        return i

    def scatter_end(u, c, p, i):
        settle(slab_in.at[u, c, p], i)
        total = slab[u, c, p, y if SPLIT[p][0] == 0 else x].astype(F32)
        for n in range(3):
            total = total + slab_in[u, c, p, n].astype(F32)
        return total

    def chain(c):
        over = spreads[c].pop()
        for d, copy in zip((1, 3, 2), spreads[c]):
            copy.wait_recv()
            from_z = (z - d + 4) % 4
            there = attn.at[c, pl.ds(2 * ((from_z % 2) * 4 + (from_z // 2) * 2 + core), 2)]
            send(there, there, across(), over)
        yield "attn"
        settle(attn.at[c, pl.ds(0, 8)], over)
        lhs = attn.at[c]
        first = []
        for p, (h, cols) in enumerate(SPLIT):
            product(c, lhs, wo, cols, part.at[0])
            first.append(scatter_out(0, c, p))
            yield f"out{p}"
        second = []
        for p in range(4):
            second.append(scatter_mid(0, c, p, first[p]))
            yield f"mid{p}"
        gathers = []
        for p, (h, cols) in enumerate(SPLIT):
            value = residual_rows[c * R:(c + 1) * R, cols].astype(F32) + scatter_end(0, c, p, second[p])
            stream[c, :, cols] = value
            rows[c, x, y, :, cols] = (value * gain[:, cols]).astype(BF)
            here = rows.at[c, x, y, :, cols]
            gathers.append(group())
            for d in (2, 1, 3):
                send(here, here, along_y(d) if h == 0 else along_x(d), gathers[p])
            yield f"stream{p}"
        wider = group()
        for p, (h, cols) in enumerate(SPLIT):
            settle(rows.at[c, 0, pl.ds(0, 3), :, cols], gathers[p])
            here = rows.at[c, x, :, :, cols] if h == 0 else rows.at[c, :, y, :, cols]
            for d in (2, 1, 3):
                send(here, here, along_x(d) if h == 0 else along_y(d), wider)
            yield f"wide{p}"
        settle(rows.at[c, pl.ds(0, 3)], wider)
        yield "rows"

        lhs = rows.at[c].reshape(16, R, FEATURES)
        crossing = []
        reduced = group()
        theirs = pl.ds(8 * (1 - core), 8)

        def cross(g):
            product(c, lhs, gu, GROUPS[g], gates)
            crossing.append(send(
                gates.at[c, theirs, :, GROUPS[g]], gates_core.at[c, :, :, GROUPS[g]], across()
            ))

        def reduce(g):
            crossing[g].wait_recv()
            for n, d in enumerate((2, 1, 3)):
                to = (z + d) % 4
                at = pl.ds(8 * core + 2 * to, 2)
                gates[c, at, :, GROUPS[g]] = (
                    gates[c, at, :, GROUPS[g]].astype(F32)
                    + gates_core[c, pl.ds(2 * to, 2), :, GROUPS[g]].astype(F32)
                ).astype(BF)
                send(
                    gates.at[c, at, :, GROUPS[g]], gates_in.at[c, n, :, :, GROUPS[g]], along_z(d), reduced
                )

        cross(0)
        yield "gate0"
        for g in range(1, len(GROUPS)):
            cross(g)
            yield f"gate{g}"
            reduce(g - 1)
            yield f"reduce{g - 1}"
        reduce(len(GROUPS) - 1)

        def square(b, carry):
            v = rows[c, b // 4, b % 4].astype(F32)
            total = jnp.sum(v * v * unscale, axis=1, keepdims=True)
            squares[c, b] = jnp.broadcast_to(total, (R, 128))
            return carry

        lax.fori_loop(0, 16, square, 0)
        squared = group()
        n = 0
        for other in (False, True):
            for d in (0, 1, 2, 3):
                if d == 0 and not other:
                    continue
                owner = (1 - core if other else core) * 4 + (z + d) % 4
                send(
                    squares.at[c, pl.ds(2 * owner, 2)], squares_in.at[c, n],
                    across() if d == 0 else along_z(d, other), squared,
                )
                n += 1
        yield "squares"
        settle(squares_in.at[c], squared)
        settle(gates_in.at[c], reduced)
        owner = 2 * (4 * core + z)
        total = squares[c, pl.ds(owner, 2)]
        for n in range(7):
            total = total + squares_in[c, n]
        scale = lax.rsqrt(total / D + EPSILON)[:, :, 0:1]

        def summed(cols):
            total = gates[c, pl.ds(owner, 2), :, cols].astype(F32)
            total = total + gates_core[c, pl.ds(2 * z, 2), :, cols].astype(F32)
            for n in range(3):
                total = total + gates_in[c, n, :, :, cols].astype(F32)
            return total * scale

        gate = summed(slice(0, HIDDEN))
        up = summed(slice(HIDDEN, 2 * HIDDEN))
        hidden[c, pl.ds(owner, 2)] = (gate / (1.0 + jnp.exp(-gate)) * up).astype(BF)
        here = hidden.at[c, pl.ds(owner, 2)]
        spread = [send(here, here, along_z(d)) for d in (2, 1, 3)]
        over = group()
        send(here, here, across(), over)
        yield "hidden"
        for d, copy in ((1, spread[1]), (3, spread[2]), (2, spread[0])):
            copy.wait_recv()
            there = hidden.at[c, pl.ds(2 * (4 * core + (z - d + 4) % 4), 2)]
            send(there, there, across(), over)
            if d != 1:
                yield "onward" if d == 3 else "over"
        settle(hidden.at[c, pl.ds(0, 8)], over)
        lhs = hidden.at[c]
        first = []
        for p, (h, cols) in enumerate(SPLIT):
            product(c, lhs, wd, cols, part.at[1])
            first.append(scatter_out(1, c, p))
            yield f"down{p}"
        second = []
        for p in range(4):
            second.append(scatter_mid(1, c, p, first[p]))
            yield f"downmid{p}"
        for p, (h, cols) in enumerate(SPLIT):
            mixed[c * R:(c + 1) * R, cols] = (
                stream[c, :, cols] + scatter_end(1, c, p, second[p])
            ).astype(BF)
            yield f"end{p}"

    chains = [chain(c) for c in range(CHUNKS)]
    for c, last in ORDER:
        if last == "unweave":
            unweave_piece(2)
            unweave_piece(3)
            raw_in[PIECES].wait()
            continue
        while next(chains[c]) != last:
            pass
    assert len(groups) == RECV_SEMS
    for copy in sent:
        copy.wait_send()


SEND_SEMS = 8
RECV_SEMS = 1 + CHUNKS * 35


def local(
    queries, cache_keys, cache_values, new_keys, new_values, lengths,
    out_weight, residual, norm_gain, gate_up, down_weight,
):
    vmem = pl.BlockSpec(memory_space=pltpu.VMEM)
    smem = pl.BlockSpec(memory_space=pltpu.SMEM)
    anywhere = pl.BlockSpec(memory_space=pl.ANY)
    return pl.pallas_call(
        kernel,
        out_shape=jax.ShapeDtypeStruct((32, FEATURES), BF),
        in_specs=[smem] + [vmem] * 4 + [anywhere] * 6,
        out_specs=vmem,
        scratch_shapes=[
            pltpu.VMEM((4, LEN, KVH * HD), BF),
            pltpu.VMEM((4, LEN, KVH * HD), BF),
            pltpu.VMEM((32, FEATURES), BF),
            pltpu.VMEM((512, FEATURES), BF),
            pltpu.VMEM((2, 2 * FEATURES // PIECES, HIDDEN), BF),
            pltpu.VMEM((FEATURES, 2 * HIDDEN), BF),
            pltpu.VMEM((HIDDEN, FEATURES), BF),
            pltpu.VMEM((4, 64, HD), F32),
            pltpu.VMEM((16, 16, HD), F32),
            pltpu.VMEM((16, 16, HD), BF),
            pltpu.VMEM((16, 16, HD), BF),
            pltpu.VMEM((CHUNKS, 16, R, 512), BF),
            pltpu.VMEM((256, 256), BF),
            pltpu.VMEM((256, 256), BF),
            pltpu.VMEM((2, CHUNKS, 16, R, FEATURES), BF),
            pltpu.VMEM((2, CHUNKS, 4, 3, 4, R, WIDE), BF),
            pltpu.VMEM((2, CHUNKS, 4, 4, R, WIDE), BF),
            pltpu.VMEM((2, CHUNKS, 4, 3, R, WIDE), BF),
            pltpu.VMEM((CHUNKS, 4, 4, R, FEATURES), BF),
            pltpu.VMEM((CHUNKS, R, FEATURES), F32),
            pltpu.VMEM((CHUNKS, 16, R, 128), F32),
            pltpu.VMEM((CHUNKS, 7, 2, R, 128), F32),
            pltpu.VMEM((CHUNKS, 16, R, 2 * HIDDEN), BF),
            pltpu.VMEM((CHUNKS, 8, R, 2 * HIDDEN), BF),
            pltpu.VMEM((CHUNKS, 3, 2, R, 2 * HIDDEN), BF),
            pltpu.VMEM((CHUNKS, 16, R, HIDDEN), BF),
            pltpu.SemaphoreType.DMA((SEND_SEMS,)),
            pltpu.SemaphoreType.DMA((RECV_SEMS,)),
            pltpu.SemaphoreType.DMA((8 + 3 + PIECES,)),
        ],
        compiler_params=pltpu.CompilerParams(
            collective_id=0, has_side_effects=True, vmem_limit_bytes=63 * 2**20,
        ),
        cost_estimate=pl.CostEstimate(
            flops=2 * 6 * 10**9, bytes_accessed=28 * 10**6, transcendentals=2 * 10**6
        ),
    )(
        lengths, queries, new_keys, new_values, norm_gain, residual,
        cache_keys, cache_values, out_weight, gate_up, down_weight,
    )


def solution(mesh):
    placed = (
        P(("sec", "grp", "shard"), None),
        P(("sec", "grp", "shard"), None, None),
        P(("sec", "grp", "shard"), None, None),
        P(("sec", "grp", "shard"), None),
        P(("sec", "grp", "shard"), None),
        P(("sec", "grp", "shard")),
        P("shard", ("sec", "grp")),
        P("shard", ("sec", "grp")),
        P(("sec", "grp")),
        P(("sec", "grp"), None, "shard"),
        P("shard", ("sec", "grp")),
    )
    return jax.shard_map(
        local, mesh=mesh, in_specs=placed, out_specs=P("shard", ("sec", "grp")), check_vma=False
    )
```

```python
import jax
import jax.numpy as jnp
from jax import lax
from jax.experimental import pallas as pl
from jax.experimental.pallas import tpu as pltpu
from jax.sharding import PartitionSpec as P

MESH = pl.DeviceIdType.MESH
BF = jnp.bfloat16
F32 = jnp.float32

D = 16384
KVH = 4
HD = 128
LEN = 512
ROWS = 512
FEATURES = 2048
HIDDEN = 1664
EPSILON = 1e-05

CHUNKS = 2
R = 32 // CHUNKS
HALF = FEATURES // 2
TILE = 256
PIECES = 4
ORDER = (
    (0, "out7"), (1, "attn"), (0, "unweave"), (1, "out0"), (0, "mid0"), (1, "out1"), (0, "mid4"),
    (1, "out2"), (0, "mid5"), (1, "out3"), (0, "mid7"), (1, "out4"), (0, "stream0"), (1, "out5"),
    (0, "stream3"), (1, "out7"), (0, "stream4"), (1, "mid2"), (0, "stream6"), (1, "mid3"),
    (0, "stream7"), (1, "mid5"), (0, "wide3"), (1, "mid7"), (0, "wide4"), (1, "stream4"),
    (0, "wide5"), (1, "stream5"), (0, "wide7"), (1, "wide5"), (0, "gate0"), (1, "wide6"),
    (0, "gate2"), (1, "wide7"), (0, "reduce3"), (1, "gate0"), (0, "squares"), (1, "squares"),
    (0, "hidden"), (1, "hidden"), (0, "down4"), (1, "onward"), (0, "down6"), (1, "over"),
    (0, "down7"), (1, "down7"), (0, "downmid0"), (1, "downmid2"), (0, "downmid4"), (1, "downmid5"),
    (0, "downmid7"), (1, "downmid7"), (0, "end0"), (1, "end1"), (0, "end1"), (1, "end2"),
    (0, "end3"), (1, "end3"), (0, "end5"), (1, "end5"), (0, "end7"), (1, "end7"),
)

WIDE = HALF // 4
SPLIT = tuple((h, slice(h * HALF + q * WIDE, h * HALF + (q + 1) * WIDE)) for q in range(4) for h in (0, 1))
GROUPS = tuple(slice(a, b) for a, b in zip((0, 512, 1024, 1792, 2560), (512, 1024, 1792, 2560, 3328)))


def kernel(
    lengths, queries, new_keys, new_values, norm_gain, residual,
    cache_keys, cache_values, out_weight, gate_up, down_weight,
    mixed,
    keys, values, residual_rows, wo, raw, gu, wd, q_rows, att, tiles, arrived, attn, unweave, regroup,
    part, part_in, slab, slab_in, rows, stream, squares, squares_in,
    gates, gates_core, gates_in, hidden,
    send_sem, recv_sem, local_sem,
):
    sec = lax.axis_index("sec")
    grp = lax.axis_index("grp")
    shard = lax.axis_index("shard")
    z = (grp // 2) * 2 + sec
    core = grp % 2
    x = shard // 4
    y = shard % 4
    block = sec * 4 + grp

    def plane(at):
        return {"shard": at}

    def along_x(d):
        return {"shard": ((x + d) % 4) * 4 + y}

    def along_y(d):
        return {"shard": x * 4 + (y + d) % 4}

    def along_z(d, other=False):
        to = (z + d) % 4
        c = 1 - core if other else core
        return {"sec": to % 2, "grp": (to // 2) * 2 + c}

    def across():
        return {"grp": (grp // 2) * 2 + (1 - core)}

    sent = []
    groups = []

    def group():
        groups.append(len(groups))
        return groups[-1]

    def send(src, dst, to, i=None):
        i = group() if i is None else i
        copy = pltpu.make_async_remote_copy(
            src_ref=src, dst_ref=dst, send_sem=send_sem.at[len(sent) % SEND_SEMS],
            recv_sem=recv_sem.at[i], device_id=to, device_id_type=MESH,
        )
        copy.start()
        sent.append(copy)
        return copy

    def settle(ref, i):
        pltpu.make_async_copy(ref, ref, recv_sem.at[i]).wait()

    fetched = []

    def fetch(src, dst):
        copy = pltpu.make_async_copy(src, dst, local_sem.at[len(fetched)])
        copy.start()
        fetched.append(copy)
        return copy

    cache = [
        (fetch(cache_keys.at[r], keys.at[r]), fetch(cache_values.at[r], values.at[r]))
        for r in range(4)
    ]
    barrier = pltpu.get_barrier_semaphore()
    for d in range(1, 16):
        pl.semaphore_signal(barrier, inc=1, device_id=plane((shard + d) % 16), device_id_type=MESH)
    for d in range(1, 4):
        pl.semaphore_signal(barrier, inc=1, device_id=along_z(d), device_id_type=MESH)
        pl.semaphore_signal(barrier, inc=1, device_id=along_z(d, True), device_id_type=MESH)
    pl.semaphore_signal(barrier, inc=1, device_id=across(), device_id_type=MESH)

    woven = gate_up.reshape(2 * FEATURES, HIDDEN)
    depth = 2 * FEATURES // PIECES

    def fetch_raw(p):
        return fetch(woven.at[pl.ds(p * depth, depth), :], raw.at[p % 2])

    def unweave_piece(p):
        raw_in[p].wait()

        def body(step, carry):
            at = pl.multiple_of(step * 256, 256)
            both = jnp.dot(
                unweave[...], raw[p % 2, pl.ds(at, 256), :], preferred_element_type=F32
            ).astype(BF)
            to = pl.ds(pl.multiple_of(p * (depth // 2) + step * 128, 128), 128)
            gu[to, 0:HIDDEN] = both[:128]
            gu[to, HIDDEN:] = both[128:]
            return carry

        lax.fori_loop(0, depth // 256, body, 0)
        if p + 2 < PIECES:
            raw_in[p + 2] = fetch_raw(p + 2)
        if p + 3 == PIECES:
            raw_in[PIECES] = fetch(down_weight, wd)

    scaling = HD ** (-0.5)
    for h in range(KVH * 16):
        q_rows[:, h, :] = queries[:, h * HD:(h + 1) * HD].astype(F32)
    own_keys = new_keys[...].astype(F32)
    own_values = new_values[...].astype(F32)
    slots = lax.broadcasted_iota(jnp.int32, (1, LEN), 1)
    for r in range(4):
        usable = slots < lengths[r]
        cache[r][0].wait()
        scores, own, own_value = [], [], []
        for k in range(KVH):
            of_head = slice(k * HD, (k + 1) * HD)
            query = q_rows[r, k * 16:(k + 1) * 16, :]
            scores.append(lax.dot_general(
                query.astype(BF), keys[r, :, of_head], (((1,), (1,)), ((), ())),
                preferred_element_type=F32,
            ))
            own.append(query * own_keys[r:r + 1, of_head])
            own_value.append(jnp.broadcast_to(own_values[r:r + 1, of_head], (16, HD)))
        scores = jnp.where(usable, jnp.concatenate(scores, axis=0) * scaling, -1e30)
        own = jnp.sum(jnp.concatenate(own, axis=0), axis=1, keepdims=True) * scaling
        top = jnp.maximum(jnp.max(scores, axis=1, keepdims=True), own)
        weights = jnp.exp(scores - top)
        own_weight = jnp.exp(own - top)
        total = jnp.sum(weights, axis=1, keepdims=True) + own_weight
        weights = weights.astype(BF)
        cache[r][1].wait()
        summed = jnp.concatenate([
            jnp.dot(
                weights[k * 16:(k + 1) * 16], values[r, :, k * HD:(k + 1) * HD],
                preferred_element_type=F32,
            ) for k in range(KVH)
        ], axis=0)
        own_low = own_weight.astype(BF).astype(F32)
        result = (summed + own_low * jnp.concatenate(own_value, axis=0)) / total
        for g in range(16):
            att[g, 4 * r:4 * r + 4, :] = result[4 * g:4 * g + 4, :]
    tiles[...] = att[...].astype(BF)

    wo_in = fetch(out_weight, wo)
    residual_in = fetch(residual, residual_rows)
    raw_in = {0: fetch_raw(0), 1: fetch_raw(1)}
    pl.semaphore_wait(barrier, 22)

    exchange = group()
    for d in range(1, 16):
        to = (shard + d) % 16
        send(tiles.at[to], arrived.at[shard], plane(to), exchange)
    arrived[shard] = tiles[shard]
    i = lax.broadcasted_iota(jnp.int32, (256, 256), 0)
    j = lax.broadcasted_iota(jnp.int32, (256, 256), 1)
    regroup[...] = jnp.where(
        j == ((i & 60) << 2) + ((i & 3) << 2) + (i >> 6), 1.0, 0.0
    ).astype(BF)
    unweave[...] = jnp.where(j == ((i & 127) << 1) + (i >> 7), 1.0, 0.0).astype(BF)
    unweave_piece(0)
    settle(arrived.at[pl.ds(0, 15)], exchange)
    grouped = jnp.dot(
        regroup[...], arrived[...].reshape(256, HD), preferred_element_type=F32
    ).astype(BF)
    for h in range(4):
        of_head = grouped[h * 64:(h + 1) * 64, :].reshape(2, CHUNKS, R, HD)
        for c in range(CHUNKS):
            attn[c, pl.ds(2 * block, 2), :, h * HD:(h + 1) * HD] = of_head[:, c]
    spreads = []
    for c in range(CHUNKS):
        mine = attn.at[c, pl.ds(2 * block, 2)]
        spreads.append([send(mine, mine, along_z(d)) for d in (1, 3, 2)])
        spreads[c].append(group())
        send(mine, mine, across(), spreads[c][-1])
    unweave_piece(1)
    wo_in.wait()
    residual_in.wait()

    gain = norm_gain[...].reshape(1, FEATURES)
    unscale = 1.0 / (gain * gain)

    def product(c, lhs, weight, half, dst):
        start = half.start
        count = (half.stop - start) // TILE

        def body(step, carry):
            at = pl.ds(pl.multiple_of(start + step * TILE, TILE), TILE)
            tile = jnp.dot(
                lhs[...].reshape(16 * R, lhs.shape[-1]), weight[:, at],
                preferred_element_type=F32,
            ).astype(BF)
            dst[c, :, :, at] = tile.reshape(16, R, TILE)
            return carry

        lax.fori_loop(0, count, body, 0)

    def scatter_out(u, c, p):
        h, cols = SPLIT[p]
        i = group()
        grid = part.at[u, c].reshape(4, 4, R, FEATURES)
        for n, d in enumerate((2, 1, 3)):
            if h == 0:
                src, to = grid.at[(x + d) % 4, :, :, cols], along_x(d)
            else:
                src, to = grid.at[:, (y + d) % 4, :, cols], along_y(d)
            send(src, part_in.at[u, c, p, n], to, i)
        return i

    def scatter_mid(u, c, p, i):
        h, cols = SPLIT[p]
        settle(part_in.at[u, c, p], i)
        grid = part.at[u, c].reshape(4, 4, R, FEATURES)
        total = (grid[x, :, :, cols] if h == 0 else grid[:, y, :, cols]).astype(F32)
        for n in range(3):
            total = total + part_in[u, c, p, n].astype(F32)
        slab[u, c, p] = total.astype(BF)
        i = group()
        for n, d in enumerate((2, 1, 3)):
            if h == 0:
                src, to = slab.at[u, c, p, (y + d) % 4], along_y(d)
            else:
                src, to = slab.at[u, c, p, (x + d) % 4], along_x(d)
            send(src, slab_in.at[u, c, p, n], to, i)
        return i

    def scatter_end(u, c, p, i):
        settle(slab_in.at[u, c, p], i)
        total = slab[u, c, p, y if SPLIT[p][0] == 0 else x].astype(F32)
        for n in range(3):
            total = total + slab_in[u, c, p, n].astype(F32)
        return total

    def chain(c):
        over = spreads[c].pop()
        for d, copy in zip((1, 3, 2), spreads[c]):
            copy.wait_recv()
            from_z = (z - d + 4) % 4
            there = attn.at[c, pl.ds(2 * ((from_z % 2) * 4 + (from_z // 2) * 2 + core), 2)]
            send(there, there, across(), over)
        yield "attn"
        settle(attn.at[c, pl.ds(0, 8)], over)
        lhs = attn.at[c]
        first = []
        for p, (h, cols) in enumerate(SPLIT):
            product(c, lhs, wo, cols, part.at[0])
            first.append(scatter_out(0, c, p))
            yield f"out{p}"
        second = []
        for p in range(len(SPLIT)):
            second.append(scatter_mid(0, c, p, first[p]))
            yield f"mid{p}"
        gathers = []
        for p, (h, cols) in enumerate(SPLIT):
            value = residual_rows[c * R:(c + 1) * R, cols].astype(F32) + scatter_end(0, c, p, second[p])
            stream[c, :, cols] = value
            rows[c, x, y, :, cols] = (value * gain[:, cols]).astype(BF)
            here = rows.at[c, x, y, :, cols]
            gathers.append(group())
            for d in (2, 1, 3):
                send(here, here, along_y(d) if h == 0 else along_x(d), gathers[p])
            yield f"stream{p}"
        wider = group()
        for p, (h, cols) in enumerate(SPLIT):
            settle(rows.at[c, 0, pl.ds(0, 3), :, cols], gathers[p])
            here = rows.at[c, x, :, :, cols] if h == 0 else rows.at[c, :, y, :, cols]
            for d in (2, 1, 3):
                send(here, here, along_x(d) if h == 0 else along_y(d), wider)
            yield f"wide{p}"
        settle(rows.at[c, pl.ds(0, 3)], wider)
        yield "rows"

        lhs = rows.at[c].reshape(16, R, FEATURES)
        crossing = []
        reduced = group()
        theirs = pl.ds(8 * (1 - core), 8)

        def cross(g):
            product(c, lhs, gu, GROUPS[g], gates)
            crossing.append(send(
                gates.at[c, theirs, :, GROUPS[g]], gates_core.at[c, :, :, GROUPS[g]], across()
            ))

        def reduce(g):
            crossing[g].wait_recv()
            for n, d in enumerate((2, 1, 3)):
                to = (z + d) % 4
                at = pl.ds(8 * core + 2 * to, 2)
                gates[c, at, :, GROUPS[g]] = (
                    gates[c, at, :, GROUPS[g]].astype(F32)
                    + gates_core[c, pl.ds(2 * to, 2), :, GROUPS[g]].astype(F32)
                ).astype(BF)
                send(
                    gates.at[c, at, :, GROUPS[g]], gates_in.at[c, n, :, :, GROUPS[g]], along_z(d), reduced
                )

        cross(0)
        yield "gate0"
        for g in range(1, len(GROUPS)):
            cross(g)
            yield f"gate{g}"
            reduce(g - 1)
            yield f"reduce{g - 1}"
        reduce(len(GROUPS) - 1)

        def square(b, carry):
            v = rows[c, b // 4, b % 4].astype(F32)
            total = jnp.sum(v * v * unscale, axis=1, keepdims=True)
            squares[c, b] = jnp.broadcast_to(total, (R, 128))
            return carry

        lax.fori_loop(0, 16, square, 0)
        squared = group()
        n = 0
        for other in (False, True):
            for d in (0, 1, 2, 3):
                if d == 0 and not other:
                    continue
                owner = (1 - core if other else core) * 4 + (z + d) % 4
                send(
                    squares.at[c, pl.ds(2 * owner, 2)], squares_in.at[c, n],
                    across() if d == 0 else along_z(d, other), squared,
                )
                n += 1
        yield "squares"
        settle(squares_in.at[c], squared)
        settle(gates_in.at[c], reduced)
        owner = 2 * (4 * core + z)
        total = squares[c, pl.ds(owner, 2)]
        for n in range(7):
            total = total + squares_in[c, n]
        scale = lax.rsqrt(total / D + EPSILON)[:, :, 0:1]

        def summed(cols):
            total = gates[c, pl.ds(owner, 2), :, cols].astype(F32)
            total = total + gates_core[c, pl.ds(2 * z, 2), :, cols].astype(F32)
            for n in range(3):
                total = total + gates_in[c, n, :, :, cols].astype(F32)
            return total * scale

        gate = summed(slice(0, HIDDEN))
        up = summed(slice(HIDDEN, 2 * HIDDEN))
        hidden[c, pl.ds(owner, 2)] = (gate / (1.0 + jnp.exp(-gate)) * up).astype(BF)
        here = hidden.at[c, pl.ds(owner, 2)]
        spread = [send(here, here, along_z(d)) for d in (2, 1, 3)]
        over = group()
        send(here, here, across(), over)
        yield "hidden"
        for d, copy in ((1, spread[1]), (3, spread[2]), (2, spread[0])):
            copy.wait_recv()
            there = hidden.at[c, pl.ds(2 * (4 * core + (z - d + 4) % 4), 2)]
            send(there, there, across(), over)
            if d != 1:
                yield "onward" if d == 3 else "over"
        settle(hidden.at[c, pl.ds(0, 8)], over)
        lhs = hidden.at[c]
        first = []
        for p, (h, cols) in enumerate(SPLIT):
            product(c, lhs, wd, cols, part.at[1])
            first.append(scatter_out(1, c, p))
            yield f"down{p}"
        second = []
        for p in range(len(SPLIT)):
            second.append(scatter_mid(1, c, p, first[p]))
            yield f"downmid{p}"
        for p, (h, cols) in enumerate(SPLIT):
            mixed[c * R:(c + 1) * R, cols] = (
                stream[c, :, cols] + scatter_end(1, c, p, second[p])
            ).astype(BF)
            yield f"end{p}"

    chains = [chain(c) for c in range(CHUNKS)]
    for c, last in ORDER:
        if last == "unweave":
            unweave_piece(2)
            unweave_piece(3)
            raw_in[PIECES].wait()
            continue
        while next(chains[c]) != last:
            pass
    assert len(groups) == RECV_SEMS
    for copy in sent:
        copy.wait_send()


SEND_SEMS = 8
RECV_SEMS = 1 + CHUNKS * (11 + 5 * len(SPLIT) + len(GROUPS))


def local(
    queries, cache_keys, cache_values, new_keys, new_values, lengths,
    out_weight, residual, norm_gain, gate_up, down_weight,
):
    vmem = pl.BlockSpec(memory_space=pltpu.VMEM)
    smem = pl.BlockSpec(memory_space=pltpu.SMEM)
    anywhere = pl.BlockSpec(memory_space=pl.ANY)
    return pl.pallas_call(
        kernel,
        out_shape=jax.ShapeDtypeStruct((32, FEATURES), BF),
        in_specs=[smem] + [vmem] * 4 + [anywhere] * 6,
        out_specs=vmem,
        scratch_shapes=[
            pltpu.VMEM((4, LEN, KVH * HD), BF),
            pltpu.VMEM((4, LEN, KVH * HD), BF),
            pltpu.VMEM((32, FEATURES), BF),
            pltpu.VMEM((512, FEATURES), BF),
            pltpu.VMEM((2, 2 * FEATURES // PIECES, HIDDEN), BF),
            pltpu.VMEM((FEATURES, 2 * HIDDEN), BF),
            pltpu.VMEM((HIDDEN, FEATURES), BF),
            pltpu.VMEM((4, 64, HD), F32),
            pltpu.VMEM((16, 16, HD), F32),
            pltpu.VMEM((16, 16, HD), BF),
            pltpu.VMEM((16, 16, HD), BF),
            pltpu.VMEM((CHUNKS, 16, R, 512), BF),
            pltpu.VMEM((256, 256), BF),
            pltpu.VMEM((256, 256), BF),
            pltpu.VMEM((2, CHUNKS, 16, R, FEATURES), BF),
            pltpu.VMEM((2, CHUNKS, len(SPLIT), 3, 4, R, WIDE), BF),
            pltpu.VMEM((2, CHUNKS, len(SPLIT), 4, R, WIDE), BF),
            pltpu.VMEM((2, CHUNKS, len(SPLIT), 3, R, WIDE), BF),
            pltpu.VMEM((CHUNKS, 4, 4, R, FEATURES), BF),
            pltpu.VMEM((CHUNKS, R, FEATURES), F32),
            pltpu.VMEM((CHUNKS, 16, R, 128), F32),
            pltpu.VMEM((CHUNKS, 7, 2, R, 128), F32),
            pltpu.VMEM((CHUNKS, 16, R, 2 * HIDDEN), BF),
            pltpu.VMEM((CHUNKS, 8, R, 2 * HIDDEN), BF),
            pltpu.VMEM((CHUNKS, 3, 2, R, 2 * HIDDEN), BF),
            pltpu.VMEM((CHUNKS, 16, R, HIDDEN), BF),
            pltpu.SemaphoreType.DMA((SEND_SEMS,)),
            pltpu.SemaphoreType.DMA((RECV_SEMS,)),
            pltpu.SemaphoreType.DMA((8 + 3 + PIECES,)),
        ],
        compiler_params=pltpu.CompilerParams(
            collective_id=0, has_side_effects=True, vmem_limit_bytes=63 * 2**20,
        ),
        cost_estimate=pl.CostEstimate(
            flops=2 * 6 * 10**9, bytes_accessed=28 * 10**6, transcendentals=2 * 10**6
        ),
    )(
        lengths, queries, new_keys, new_values, norm_gain, residual,
        cache_keys, cache_values, out_weight, gate_up, down_weight,
    )


def solution(mesh):
    placed = (
        P(("sec", "grp", "shard"), None),
        P(("sec", "grp", "shard"), None, None),
        P(("sec", "grp", "shard"), None, None),
        P(("sec", "grp", "shard"), None),
        P(("sec", "grp", "shard"), None),
        P(("sec", "grp", "shard")),
        P("shard", ("sec", "grp")),
        P("shard", ("sec", "grp")),
        P(("sec", "grp")),
        P(("sec", "grp"), None, "shard"),
        P("shard", ("sec", "grp")),
    )
    return jax.shard_map(
        local, mesh=mesh, in_specs=placed, out_specs=P("shard", ("sec", "grp")), check_vma=False
    )
```
